256 devices in a mesh: tm: 16 (over z, core), chan: 16 (over x, y).
Axes of the slice: x: 4, y: 4, z: 8, core: 2. Of those that a mesh axis runs over, the one named last changes fastest.
Arguments:
- latent: bfloat16 [32, 1024, 16, 4], P('tm', 'chan'), may hold values from -81 to 81
- conv_first: bfloat16 [1024, 27, 1024], P('chan'), may hold values from -0.0390625 to 0.0390625
- conv_second: bfloat16 [1024, 27, 1024], P('chan'), may hold values from -0.0390625 to 0.0390625
- conv_upsample: bfloat16 [27, 1024, 4096], P(None, 'chan', 'tm'), may hold values from -0.0390625 to 0.0390625
Outputs:
- upsampled: bfloat16 [32, 512, 512], P('chan', 'tm')
The draws below stay inside these ranges and needn't reach their ends.
All inputs are finite; a program needn't handle non-finite values.
Results may differ from the reference program's by a relative error of at most 0.0051.
Values may be sent and summed in bfloat16 or wider, within the bound.
No kernel may reach another device: no remote copies, remote signals or barrier semaphores. Data moves between devices by JAX's collectives and lax.ppermute only.
A program may use at most 128 MiB of HBM per device.

```python
import jax
import jax.numpy as jnp
from jax import lax

D = 1024
OUTC = 512
WIDE = 4
FRAMES = 32
ROWS = 16


def draw_latent(key, part):
    key = jax.random.fold_in(key, 11)
    keys = jax.random.split(key, 3)
    shape = (FRAMES, D, ROWS, WIDE)
    position = jnp.arange(D, dtype=jnp.float32) / D
    base = jnp.clip(jax.random.normal(keys[0], shape, jnp.float32), -3.0, 3.0)
    ramp = jnp.exp(position * jnp.log(3.0))
    scales = jnp.exp(jax.random.uniform(keys[1], (D,), jnp.float32, jnp.log(0.2), jnp.log(2.0)))
    spots = jnp.exp(jax.random.uniform(keys[2], (FRAMES, 1, ROWS, WIDE), jnp.float32, jnp.log(0.3), jnp.log(3.0)))
    return (base * (scales * ramp)[None, :, None, None] * spots).astype(jnp.bfloat16)


def block_scale(own_key, extent, shards, least, high):
    gain = 1.0
    for dim, shards_of in shards:
        heights = jax.random.uniform(jax.random.fold_in(jax.random.fold_in(own_key, 6), dim), (shards_of,), jnp.float32, least / len(shards), high / len(shards))
        gain = gain * jnp.repeat(jnp.exp(heights), extent[dim] // shards_of).reshape((-1,) + (1,) * (len(extent) - 1 - dim))
    return gain


def normal_values(own_key, dims, width, most, shards=(), kind=jnp.bfloat16):
    gain = block_scale(own_key, dims, shards, -0.22, 0.18) if shards else 1.0
    entries = jax.random.normal(own_key, dims, jnp.float32) * width * gain
    return jnp.minimum(jnp.maximum(entries, -most), most).astype(kind)


def setup_inputs(seed: int = 0) -> dict:
    seeds = jax.random.split(jax.random.key(seed), 5)
    return {
        "latent": draw_latent(jax.random.fold_in(seeds[4], 71), 0),
        "conv_first": normal_values(seeds[1], (D, 27, D), (27 * D) ** -0.5, 0.0390625, ((0, 16),)),
        "conv_second": normal_values(seeds[2], (D, 27, D), (27 * D) ** -0.5, 0.0390625, ((0, 16),)),
        "conv_upsample": normal_values(seeds[3], (27, D, 8 * OUTC), (27 * D) ** -0.5, 0.0390625, ((1, 16), (2, 16))),
    }


def pad_time(values):
    return jnp.concatenate([values[:1], values[:1], values], 0)

def pixel_act(values):
    floats = values.astype(jnp.float32)
    squares = lax.optimization_barrier(jnp.mean(floats * floats, axis=1, keepdims=True))
    return jax.nn.silu(floats * jax.lax.rsqrt(squares + 1e-06)).astype(jnp.bfloat16)

def convolve_block(window, weight):
    frames = window.shape[0] - 2
    rows = window.shape[2]
    columns = window.shape[3]
    padded = jnp.pad(window, ((0, 0), (0, 0), (1, 1), (1, 1)))
    total = jnp.zeros((frames, weight.shape[0], rows, columns), jnp.float32)
    for frame_off in range(3):
        for row_off in range(3):
            for col_off in range(3):
                tap_index = 9 * frame_off + 3 * row_off + col_off
                tapped = padded[frame_off:frame_off + frames, :, row_off:row_off + rows, col_off:col_off + columns].astype(jnp.float32)
                total = total + jnp.einsum('tchw,oc->tohw', tapped, weight[:, tap_index, :].astype(jnp.float32))
    return total

def convolve_upsample(window, weight):
    frames = window.shape[0] - 2
    rows = window.shape[2]
    columns = window.shape[3]
    padded = jnp.pad(window, ((0, 0), (0, 0), (1, 1), (1, 1)))
    total = jnp.zeros((frames, weight.shape[2], rows, columns), jnp.float32)
    for frame_off in range(3):
        for row_off in range(3):
            for col_off in range(3):
                tap_index = 9 * frame_off + 3 * row_off + col_off
                tapped = padded[frame_off:frame_off + frames, :, row_off:row_off + rows, col_off:col_off + columns].astype(jnp.float32)
                total = total + jnp.einsum('tchw,co->tohw', tapped, weight[tap_index].astype(jnp.float32))
    return total

def depth_space(expanded):
    frames, channels, rows, columns = expanded.shape
    grouped = expanded.reshape(frames, channels // 8, 2, 2, 2, rows, columns)
    grouped = jnp.transpose(grouped, (5, 3, 1, 0, 2, 6, 4))
    return grouped.reshape(2 * rows, channels // 8, 4 * frames * columns)

def reference(latent, conv_first, conv_second, conv_upsample):
    first_act = pixel_act(latent)
    hidden = convolve_block(pad_time(first_act), conv_first).astype(jnp.bfloat16)
    second_act = pixel_act(hidden)
    block_out = (latent.astype(jnp.float32) + convolve_block(pad_time(second_act), conv_second)).astype(jnp.bfloat16)
    expanded = convolve_upsample(pad_time(block_out), conv_upsample).astype(jnp.bfloat16)
    return depth_space(expanded)
```

```python
import functools

import jax
import jax.numpy as jnp
from jax import lax
from jax.experimental import pallas as pl
from jax.experimental.pallas import tpu as pltpu
from jax.sharding import PartitionSpec as P

EPSILON = 1e-06
F32 = jnp.float32
BF16 = jnp.bfloat16
COLS = 4
FRAMES = 2
CELL = FRAMES * COLS
LANES = 128
ROWS = 16
MIB = 1 << 20


def lane_ids():
    lane = lax.broadcasted_iota(jnp.int32, (1, LANES), 1)
    return lane // CELL, (lane // COLS) % FRAMES, lane % COLS


def spatial_sum(product, first_tap, outs):
    row, _, col = lane_ids()
    total = None
    for row_off in range(3):
        part = None
        for col_off in range(3):
            start = (first_tap + 3 * row_off + col_off) * outs
            piece = product[start : start + outs]
            if col_off == 0:
                piece = jnp.where(col >= 1, pltpu.roll(piece, 1, 1), 0.0)
            if col_off == 2:
                piece = jnp.where(col < COLS - 1, pltpu.roll(piece, LANES - 1, 1), 0.0)
            part = piece if part is None else part + piece
        if row_off == 0:
            part = jnp.where(row >= 1, pltpu.roll(part, CELL, 1), 0.0)
        if row_off == 2:
            part = jnp.where(row < ROWS - 1, pltpu.roll(part, LANES - CELL, 1), 0.0)
        total = part if total is None else total + part
    return total


def block_kernel(whole_ref, weight_ref, own_ref, later_ref):
    depth = whole_ref.shape[0]
    outs = own_ref.shape[0]
    values = whole_ref[...].astype(F32)
    squares = jnp.sum(values * values, axis=0, keepdims=True)
    scaled = values * lax.rsqrt(squares / depth + EPSILON)
    act = (scaled / (1.0 + jnp.exp(-scaled))).astype(BF16)
    product = jnp.dot(weight_ref[...], act, preferred_element_type=F32)
    frame = lane_ids()[1]
    oldest = spatial_sum(product, 0, outs)
    middle = spatial_sum(product, 9, outs)
    newest = spatial_sum(product, 18, outs)
    first = lax.axis_index("tm") == 0
    start = jnp.where(frame == 0, middle + oldest, pltpu.roll(oldest, COLS, 1))
    own = newest + jnp.where(frame == 1, pltpu.roll(middle, COLS, 1), 0.0)
    own_ref[...] = own + jnp.where(first, start, 0.0)
    later_ref[...] = oldest + jnp.where(frame == 0, pltpu.roll(middle, LANES - COLS, 1), 0.0)


def block_conv(whole, weight, outs):
    shape = jax.ShapeDtypeStruct((outs, LANES), F32)
    own, later = pl.pallas_call(
        block_kernel,
        out_shape=(shape, shape),
        compiler_params=pltpu.CompilerParams(vmem_limit_bytes=40 * MIB),
    )(whole, weight)
    devices = lax.axis_size("tm")
    earlier = lax.ppermute(later, "tm", [(i, i + 1) for i in range(devices - 1)])
    return own + earlier


def gathered(value, axis):
    copies = jnp.broadcast_to(value, (lax.axis_size(axis),) + value.shape)
    return lax.all_to_all(copies, axis, 0, 0, tiled=True)


def upsample_kernel(all_ref, weight_ref, out_ref, shifted):
    count, depth, _ = all_ref.shape
    lane = lax.broadcasted_iota(jnp.int32, (1, LANES), 1)
    col = lane % COLS
    blocks = [all_ref[i].astype(F32) for i in range(count)]
    bit = 1
    while bit < count:
        step = bit * CELL
        upper = (lane // step) % 2 == 1
        swapped = list(blocks)
        for i in range(count):
            if i & bit == 0:
                low, high = blocks[i], blocks[i | bit]
                swapped[i] = jnp.where(upper, pltpu.roll(high, step, 1), low)
                swapped[i | bit] = jnp.where(upper, high, pltpu.roll(low, LANES - step, 1))
        blocks = swapped
        bit *= 2
    zero = jnp.zeros((depth, LANES), BF16)
    for k in range(9):
        shifted[k, 0] = zero
        shifted[k, count + 1] = zero
    for r in range(count):
        value = blocks[r]
        back = jnp.where(lane < COLS, value, pltpu.roll(value, COLS, 1))
        back_two = jnp.where(lane < COLS, value, pltpu.roll(back, COLS, 1))
        for frame_off, moved in enumerate((back_two, back, value)):
            left = jnp.where(col >= 1, pltpu.roll(moved, 1, 1), 0.0)
            right = jnp.where(col < COLS - 1, pltpu.roll(moved, LANES - 1, 1), 0.0)
            shifted[3 * frame_off, r + 1] = left.astype(BF16)
            shifted[3 * frame_off + 1, r + 1] = moved.astype(BF16)
            shifted[3 * frame_off + 2, r + 1] = right.astype(BF16)
    pair = 2
    for r in range(0, count, pair):
        columns = []
        for j in range(pair):
            columns.append(
                jnp.concatenate(
                    [
                        shifted[3 * kt + ks, r + j + kr]
                        for kt in range(3)
                        for kr in range(3)
                        for ks in range(3)
                    ],
                    axis=0,
                )
            )
        spread = jnp.concatenate(columns, axis=1)
        result = lax.dot_general(
            weight_ref[...], spread, (((0,), (0,)), ((), ())), preferred_element_type=F32
        ).astype(BF16)
        for j in range(pair):
            out_ref[r + j] = result[:, j * LANES : (j + 1) * LANES]


def finish_kernel(parts_ref, out_ref, total_ref):
    count = parts_ref.shape[0]
    channels = out_ref.shape[1]
    total = parts_ref[0].astype(F32)
    for i in range(1, count):
        total = total + parts_ref[i].astype(F32)
    total_ref[...] = total
    wide = out_ref.shape[2]
    source = lax.broadcasted_iota(jnp.int32, (LANES, wide), 0)
    target = lax.broadcasted_iota(jnp.int32, (LANES, wide), 1)
    base = (source // COLS) * (4 * COLS) + (source % COLS) * 2
    for p2 in range(2):
        result = jnp.zeros((channels, wide), F32)
        for p1 in range(2):
            for p3 in range(2):
                rows = total_ref[pl.ds(4 * p1 + 2 * p2 + p3, channels, stride=8), :]
                place = jnp.where(target == base + 2 * COLS * p1 + p3, 1.0, 0.0).astype(BF16)
                result = result + jnp.dot(rows.astype(BF16), place, preferred_element_type=F32)
        out_ref[p2] = result.astype(BF16)


def on_device(latent, conv_first, conv_second, conv_upsample):
    channels = latent.shape[1]
    places = jnp.transpose(latent, (1, 2, 0, 3)).reshape(channels, LANES)

    def taps(weight):
        outs, count, depth = weight.shape
        return jnp.transpose(weight, (1, 0, 2)).reshape(count * outs, depth)

    whole = gathered(places, "chan").reshape(-1, LANES)
    hidden = block_conv(whole, taps(conv_first), channels).astype(BF16)
    whole = gathered(hidden, "chan").reshape(-1, LANES)
    block = block_conv(whole, taps(conv_second), channels)
    block_out = (places.astype(F32) + block).astype(BF16)
    frames = gathered(block_out, "tm")
    count = frames.shape[0]
    outs = conv_upsample.shape[2]
    partial = pl.pallas_call(
        upsample_kernel,
        out_shape=jax.ShapeDtypeStruct((count, outs, LANES), BF16),
        scratch_shapes=[pltpu.VMEM((9, count + 2, channels, LANES), BF16)],
        compiler_params=pltpu.CompilerParams(vmem_limit_bytes=40 * MIB),
    )(frames, conv_upsample.reshape(-1, outs))
    parts = lax.all_to_all(partial, "chan", 0, 0, tiled=True)
    return pl.pallas_call(
        finish_kernel,
        out_shape=jax.ShapeDtypeStruct((2, outs // 8, 4 * LANES), BF16),
        scratch_shapes=[pltpu.VMEM((outs, LANES), F32)],
        compiler_params=pltpu.CompilerParams(vmem_limit_bytes=40 * MIB),
    )(parts)


def solution(mesh):
    placed = (
        P("tm", "chan", None, None),
        P("chan", None, None),
        P("chan", None, None),
        P(None, "chan", "tm"),
    )
    return jax.shard_map(
        on_device, mesh=mesh, in_specs=placed, out_specs=P("chan", "tm", None), check_vma=False
    )
```

```python
import functools

import jax
import jax.numpy as jnp
from jax import lax
from jax.experimental import pallas as pl
from jax.experimental.pallas import tpu as pltpu
from jax.sharding import PartitionSpec as P

EPSILON = 1e-06
F32 = jnp.float32
BF16 = jnp.bfloat16
COLS = 4
FRAMES = 2
CELL = FRAMES * COLS
LANES = 128
ROWS = 16
MIB = 1 << 20


def lane_ids():
    lane = lax.broadcasted_iota(jnp.int32, (1, LANES), 1)
    return lane // CELL, (lane // COLS) % FRAMES, lane % COLS


def spatial_sum(product, first_tap, outs):
    row, _, col = lane_ids()
    total = None
    for row_off in range(3):
        part = None
        for col_off in range(3):
            start = (first_tap + 3 * row_off + col_off) * outs
            piece = product[start : start + outs]
            if col_off == 0:
                piece = jnp.where(col >= 1, pltpu.roll(piece, 1, 1), 0.0)
            if col_off == 2:
                piece = jnp.where(col < COLS - 1, pltpu.roll(piece, LANES - 1, 1), 0.0)
            part = piece if part is None else part + piece
        if row_off == 0:
            part = jnp.where(row >= 1, pltpu.roll(part, CELL, 1), 0.0)
        if row_off == 2:
            part = jnp.where(row < ROWS - 1, pltpu.roll(part, LANES - CELL, 1), 0.0)
        total = part if total is None else total + part
    return total


def start_kernel(latent_ref, places_ref, copies_ref):
    cells = [latent_ref[t, r] for r in range(ROWS) for t in range(FRAMES)]
    places = jnp.concatenate(cells, axis=0).astype(F32).T.astype(BF16)
    places_ref[...] = places
    for i in range(copies_ref.shape[0]):
        copies_ref[i] = places


def block_kernel(whole_ref, weight_ref, own_ref, later_ref):
    depth = whole_ref.shape[0]
    outs = own_ref.shape[0]
    values = whole_ref[...].astype(F32)
    squares = jnp.sum(values * values, axis=0, keepdims=True)
    scaled = values * lax.rsqrt(squares / depth + EPSILON)
    act = (scaled / (1.0 + jnp.exp(-scaled))).astype(BF16)
    product = jnp.dot(weight_ref[...], act, preferred_element_type=F32)
    frame = lane_ids()[1]
    oldest = spatial_sum(product, 0, outs)
    middle = spatial_sum(product, 9, outs)
    newest = spatial_sum(product, 18, outs)
    first = lax.axis_index("tm") == 0
    start = jnp.where(frame == 0, middle + oldest, pltpu.roll(oldest, COLS, 1))
    own = newest + jnp.where(frame == 1, pltpu.roll(middle, COLS, 1), 0.0)
    own_ref[...] = own + jnp.where(first, start, 0.0)
    later_ref[...] = oldest + jnp.where(frame == 0, pltpu.roll(middle, LANES - COLS, 1), 0.0)


def block_conv(whole, weight, outs):
    shape = jax.ShapeDtypeStruct((outs, LANES), F32)
    own, later = pl.pallas_call(
        block_kernel,
        out_shape=(shape, shape),
        compiler_params=pltpu.CompilerParams(vmem_limit_bytes=16 * MIB),
        cost_estimate=pl.CostEstimate(flops=4 * 10**9, bytes_accessed=8 * MIB, transcendentals=0),
    )(whole, weight)
    devices = lax.axis_size("tm")
    earlier = lax.ppermute(later, "tm", [(i, (i + 1) % devices) for i in range(devices)])
    return own, earlier


def join_kernel(own_ref, earlier_ref, *rest):
    copies_ref = rest[-1]
    value = own_ref[...] + jnp.where(lax.axis_index("tm") == 0, 0.0, earlier_ref[...])
    for ref in rest[:-1]:
        value = ref[...].astype(F32) + value
    value = value.astype(BF16)
    for i in range(copies_ref.shape[0]):
        copies_ref[i] = value


def joined(parts, axis):
    shape = (lax.axis_size(axis),) + parts[0].shape
    copies = pl.pallas_call(
        join_kernel,
        out_shape=jax.ShapeDtypeStruct(shape, BF16),
        compiler_params=pltpu.CompilerParams(vmem_limit_bytes=8 * MIB),
        cost_estimate=pl.CostEstimate(flops=8 * 10**9, bytes_accessed=MIB, transcendentals=0),
    )(*parts)
    return lax.all_to_all(copies, axis, 0, 0, tiled=True)


def upsample_kernel(all_ref, weight_ref, out_ref, shifted):
    count, depth, _ = all_ref.shape
    lane = lax.broadcasted_iota(jnp.int32, (1, LANES), 1)
    col = lane % COLS
    blocks = [all_ref[i].astype(F32) for i in range(count)]
    bit = 1
    while bit < count:
        step = bit * CELL
        upper = (lane // step) % 2 == 1
        swapped = list(blocks)
        for i in range(count):
            if i & bit == 0:
                low, high = blocks[i], blocks[i | bit]
                swapped[i] = jnp.where(upper, pltpu.roll(high, step, 1), low)
                swapped[i | bit] = jnp.where(upper, high, pltpu.roll(low, LANES - step, 1))
        blocks = swapped
        bit *= 2
    zero = jnp.zeros((depth, LANES), BF16)
    for k in range(9):
        shifted[k, 0] = zero
        shifted[k, count + 1] = zero
    for r in range(count):
        value = blocks[r]
        back = jnp.where(lane < COLS, value, pltpu.roll(value, COLS, 1))
        back_two = jnp.where(lane < COLS, value, pltpu.roll(back, COLS, 1))
        for frame_off, moved in enumerate((back_two, back, value)):
            left = jnp.where(col >= 1, pltpu.roll(moved, 1, 1), 0.0)
            right = jnp.where(col < COLS - 1, pltpu.roll(moved, LANES - 1, 1), 0.0)
            shifted[3 * frame_off, r + 1] = left.astype(BF16)
            shifted[3 * frame_off + 1, r + 1] = moved.astype(BF16)
            shifted[3 * frame_off + 2, r + 1] = right.astype(BF16)
    pair = 2
    for r in range(0, count, pair):
        columns = []
        for j in range(pair):
            columns.append(
                jnp.concatenate(
                    [
                        shifted[3 * kt + ks, r + j + kr]
                        for kt in range(3)
                        for kr in range(3)
                        for ks in range(3)
                    ],
                    axis=0,
                )
            )
        spread = jnp.concatenate(columns, axis=1)
        result = lax.dot_general(
            weight_ref[...], spread, (((0,), (0,)), ((), ())), preferred_element_type=F32
        ).astype(BF16)
        for j in range(pair):
            out_ref[r + j] = result[:, j * LANES : (j + 1) * LANES]


def finish_kernel(parts_ref, out_ref, total_ref):
    count = parts_ref.shape[0]
    channels = out_ref.shape[1]
    total = parts_ref[0].astype(F32)
    for i in range(1, count):
        total = total + parts_ref[i].astype(F32)
    total_ref[...] = total
    wide = out_ref.shape[2]
    source = lax.broadcasted_iota(jnp.int32, (LANES, wide), 0)
    target = lax.broadcasted_iota(jnp.int32, (LANES, wide), 1)
    base = (source // COLS) * (4 * COLS) + (source % COLS) * 2
    for p2 in range(2):
        result = jnp.zeros((channels, wide), F32)
        for p1 in range(2):
            for p3 in range(2):
                rows = total_ref[pl.ds(4 * p1 + 2 * p2 + p3, channels, stride=8), :]
                place = jnp.where(target == base + 2 * COLS * p1 + p3, 1.0, 0.0).astype(BF16)
                result = result + jnp.dot(rows.astype(BF16), place, preferred_element_type=F32)
        out_ref[p2] = result.astype(BF16)


def on_device(latent, conv_first, conv_second, conv_upsample):
    channels = latent.shape[1]
    shape = (channels, LANES)
    places, copies = pl.pallas_call(
        start_kernel,
        out_shape=(
            jax.ShapeDtypeStruct(shape, BF16),
            jax.ShapeDtypeStruct((lax.axis_size("chan"),) + shape, BF16),
        ),
        compiler_params=pltpu.CompilerParams(vmem_limit_bytes=8 * MIB),
        cost_estimate=pl.CostEstimate(flops=8 * 10**9, bytes_accessed=MIB, transcendentals=0),
    )(jnp.transpose(latent, (0, 2, 3, 1)))

    def taps(weight):
        outs, count, depth = weight.shape
        return jnp.transpose(weight, (1, 0, 2)).reshape(count * outs, depth)

    whole = lax.all_to_all(copies, "chan", 0, 0, tiled=True).reshape(-1, LANES)
    parts = block_conv(whole, taps(conv_first), channels)
    whole = joined(parts, "chan").reshape(-1, LANES)
    parts = block_conv(whole, taps(conv_second), channels)
    frames = joined((*parts, places), "tm")
    count = frames.shape[0]
    outs = conv_upsample.shape[2]
    partial = pl.pallas_call(
        upsample_kernel,
        out_shape=jax.ShapeDtypeStruct((count, outs, LANES), BF16),
        scratch_shapes=[pltpu.VMEM((9, count + 2, channels, LANES), BF16)],
        compiler_params=pltpu.CompilerParams(vmem_limit_bytes=16 * MIB),
    )(frames, conv_upsample.reshape(-1, outs))
    parts = lax.all_to_all(partial, "chan", 0, 0, tiled=True)
    return pl.pallas_call(
        finish_kernel,
        out_shape=jax.ShapeDtypeStruct((2, outs // 8, 4 * LANES), BF16),
        scratch_shapes=[pltpu.VMEM((outs, LANES), F32)],
        compiler_params=pltpu.CompilerParams(vmem_limit_bytes=16 * MIB),
    )(parts)


def solution(mesh):
    placed = (
        P("tm", "chan", None, None),
        P("chan", None, None),
        P("chan", None, None),
        P(None, "chan", "tm"),
    )
    return jax.shard_map(
        on_device, mesh=mesh, in_specs=placed, out_specs=P("chan", "tm", None), check_vma=False
    )
```

```python
import jax
import jax.numpy as jnp
import numpy as np
from jax import lax
from jax.experimental import pallas as pl
from jax.experimental.pallas import tpu as pltpu
from jax.sharding import PartitionSpec as P

EPSILON = 1e-06
F32 = jnp.float32
BF16 = jnp.bfloat16
COLS = 4
FRAMES = 2
CELL = FRAMES * COLS
LANES = 128
ROWS = 16
PAIR = 4
BAND = 4
BANDS = 2
MIB = 1 << 20


def lane_ids():
    lane = lax.broadcasted_iota(jnp.int32, (1, LANES), 1)
    return lane // CELL, (lane // COLS) % FRAMES, lane % COLS


def spatial_sum(product, first_tap, outs):
    row, _, col = lane_ids()
    total = None
    for row_off in range(3):
        part = None
        for col_off in range(3):
            start = (first_tap + 3 * row_off + col_off) * outs
            piece = product[start : start + outs]
            if col_off == 0:
                piece = jnp.where(col >= 1, pltpu.roll(piece, 1, 1), 0.0)
            if col_off == 2:
                piece = jnp.where(col < COLS - 1, pltpu.roll(piece, LANES - 1, 1), 0.0)
            part = piece if part is None else part + piece
        if row_off == 0:
            part = jnp.where(row >= 1, pltpu.roll(part, CELL, 1), 0.0)
        if row_off == 2:
            part = jnp.where(row < ROWS - 1, pltpu.roll(part, LANES - CELL, 1), 0.0)
        total = part if total is None else total + part
    return total


def start_kernel(latent_ref, places_ref, copies_ref):
    cells = [latent_ref[t, r] for r in range(ROWS) for t in range(FRAMES)]
    places = jnp.concatenate(cells, axis=0).astype(F32).T.astype(BF16)
    places_ref[...] = places
    for i in range(copies_ref.shape[0]):
        copies_ref[i] = places


def block_kernel(whole_ref, weight_ref, *rest):
    *residual, own_ref, later_ref = rest
    depth = whole_ref.shape[0]
    outs = own_ref.shape[0]
    values = whole_ref[...].astype(F32)
    squares = jnp.sum(values * values, axis=0, keepdims=True)
    scaled = values * lax.rsqrt(squares / depth + EPSILON)
    act = (scaled / (1.0 + jnp.exp(-scaled))).astype(BF16)
    product = jnp.dot(weight_ref[...], act, preferred_element_type=F32)
    frame = lane_ids()[1]
    oldest = spatial_sum(product, 0, outs)
    middle = spatial_sum(product, 9, outs)
    newest = spatial_sum(product, 18, outs)
    first = lax.axis_index("tm") == 0
    start = jnp.where(frame == 0, middle + oldest, pltpu.roll(oldest, COLS, 1))
    own = newest + jnp.where(frame == 1, pltpu.roll(middle, COLS, 1), 0.0)
    own = own + jnp.where(first, start, 0.0)
    for ref in residual:
        own = ref[...].astype(F32) + own
    own_ref[...] = own
    later_ref[...] = oldest + jnp.where(frame == 0, pltpu.roll(middle, LANES - COLS, 1), 0.0)


def block_conv(whole, weight, outs, *residual):
    shape = jax.ShapeDtypeStruct((outs, LANES), F32)
    return pl.pallas_call(
        block_kernel,
        out_shape=(shape, shape),
        compiler_params=pltpu.CompilerParams(vmem_limit_bytes=16 * MIB),
        cost_estimate=pl.CostEstimate(flops=4 * 10**9, bytes_accessed=8 * MIB, transcendentals=0),
    )(whole, weight, *residual)


def next_frames(i):
    return (i + 1) % lax.axis_size("tm")


def shifted_on(later):
    return lax.ppermute(later, "tm", [(i, next_frames(i)) for i in range(lax.axis_size("tm"))])


def swapped(value):
    return lax.ppermute(value, "chan", [(c, c ^ PAIR) for c in range(lax.axis_size("chan"))])


def shifted_and_swapped(later):
    frames, channels = lax.axis_size("tm"), lax.axis_size("chan")
    pairs = [
        (i * channels + c, next_frames(i) * channels + (c ^ PAIR))
        for i in range(frames)
        for c in range(channels)
    ]
    return lax.ppermute(later, ("tm", "chan"), pairs)


def summed(own_ref, earlier_ref):
    earlier = jnp.where(lax.axis_index("tm") == 0, 0.0, earlier_ref[...])
    return (own_ref[...] + earlier).astype(BF16)


def hidden_kernel(own_ref, earlier_ref, copies_ref):
    value = summed(own_ref, earlier_ref)
    for i in range(copies_ref.shape[0]):
        copies_ref[i] = value


def bands_kernel(own_ref, earlier_ref, own_too_ref, earlier_too_ref, copies_ref, padded):
    both = [summed(own_ref, earlier_ref), summed(own_too_ref, earlier_too_ref)]
    edge = jnp.zeros((CELL, padded.shape[1]), F32)
    padded[0:CELL] = edge
    padded[CELL + LANES :] = edge
    padded[CELL : CELL + LANES] = jnp.concatenate([v.astype(F32).T for v in both], axis=1)
    half = (lax.axis_index("chan") // PAIR) % 2
    bands = []
    for band in range(BANDS):
        first = pl.multiple_of((BAND * half + 2 * BAND * band) * CELL, CELL)
        bands.append(padded[pl.ds(first, (BAND + 2) * CELL), :])
    value = jnp.concatenate(bands, axis=0).astype(BF16)
    for i in range(copies_ref.shape[0]):
        copies_ref[i] = value


def hint(limit):
    return {
        "compiler_params": pltpu.CompilerParams(vmem_limit_bytes=limit * MIB),
        "cost_estimate": pl.CostEstimate(flops=8 * 10**9, bytes_accessed=MIB, transcendentals=0),
    }


def upsample_kernel(all_ref, move_ref, weight_ref, weight_too_ref, out_ref, moved):
    count = 2 * all_ref.shape[1]
    channels = all_ref.shape[3]
    rows = BAND + 2
    for band in range(BANDS):
        for row in range(0, rows, 2):
            places = []
            for r in (row, row + 1):
                start = (band * rows + r) * CELL
                places.append(
                    jnp.concatenate(
                        [all_ref[i % 2, i // 2, start : start + CELL].astype(F32) for i in range(count)],
                        axis=0,
                    )
                )
            pair = jnp.concatenate(places, axis=1).astype(BF16)
            result = jnp.dot(move_ref[...], pair, preferred_element_type=F32).astype(BF16)
            for k in range(9):
                for j in range(2):
                    moved[k, band, (row + j) * LANES : (row + j + 1) * LANES] = result[
                        k * LANES : (k + 1) * LANES, j * channels : (j + 1) * channels
                    ]
    blocks = []
    for tap in range(27):
        blocks.append(weight_ref[tap])
        blocks.append(weight_too_ref[tap])
    weight = jnp.concatenate(blocks, axis=0)
    for band in range(BANDS):
        spread = jnp.concatenate(
            [
                moved[3 * kt + ks, band, kr * LANES : (kr + BAND) * LANES]
                for kt in range(3)
                for kr in range(3)
                for ks in range(3)
            ],
            axis=1,
        )
        result = jnp.dot(spread, weight, preferred_element_type=F32).astype(BF16)
        for r in range(BAND):
            out_ref[band * BAND + r] = result[r * LANES : (r + 1) * LANES]


def moves():
    place = np.arange(LANES)
    frame, col = place // COLS, place % COLS
    blocks = []
    for frame_off in range(3):
        for col_off in range(3):
            target = col + col_off - 1
            source = np.maximum(frame + frame_off - 2, 0) * COLS + target
            fits = (target >= 0) & (target < COLS)
            blocks.append(fits[:, None] & (source[:, None] == place[None, :]))
    return np.concatenate(blocks, axis=0).astype(jnp.bfloat16)


def finish_kernel(parts_ref, out_ref, total_ref):
    count = parts_ref.shape[0]
    channels = out_ref.shape[1]
    total = parts_ref[0].astype(F32)
    for i in range(1, count):
        total = total + parts_ref[i].astype(F32)
    total_ref[...] = total.T
    wide = out_ref.shape[2]
    source = lax.broadcasted_iota(jnp.int32, (LANES, wide), 0)
    target = lax.broadcasted_iota(jnp.int32, (LANES, wide), 1)
    base = (source // COLS) * (4 * COLS) + (source % COLS) * 2
    for p2 in range(2):
        result = jnp.zeros((channels, wide), F32)
        for p1 in range(2):
            for p3 in range(2):
                rows = total_ref[pl.ds(4 * p1 + 2 * p2 + p3, channels, stride=8), :]
                place = jnp.where(target == base + 2 * COLS * p1 + p3, 1.0, 0.0).astype(BF16)
                result = result + jnp.dot(rows.astype(BF16), place, preferred_element_type=F32)
        out_ref[p2] = result.astype(BF16)


def on_device(latent, conv_first, conv_second, conv_upsample):
    channels = latent.shape[1]
    frames_on, channels_on = lax.axis_size("tm"), lax.axis_size("chan")

    def taps(weight):
        outs, count, depth = weight.shape
        return jnp.transpose(weight, (1, 0, 2)).reshape(count * outs, depth)

    shape = (channels, LANES)
    places, copies = pl.pallas_call(
        start_kernel,
        out_shape=(
            jax.ShapeDtypeStruct(shape, BF16),
            jax.ShapeDtypeStruct((channels_on,) + shape, BF16),
        ),
        **hint(8),
    )(jnp.transpose(latent, (0, 2, 3, 1)))
    whole = lax.all_to_all(copies, "chan", 0, 0, tiled=True).reshape(-1, LANES)

    own, later = block_conv(whole, taps(conv_first), channels)
    copies = pl.pallas_call(
        hidden_kernel, out_shape=jax.ShapeDtypeStruct((channels_on,) + shape, BF16), **hint(8)
    )(own, shifted_on(later))
    whole = lax.all_to_all(copies, "chan", 0, 0, tiled=True).reshape(-1, LANES)

    own, later = block_conv(whole, taps(conv_second), channels, places)
    own_too = swapped(own)
    earlier_too = shifted_and_swapped(later)
    earlier = shifted_on(later)
    earlier, other = lax.optimization_barrier((earlier, conv_upsample))
    other = swapped(other)
    packed = (BANDS * (BAND + 2) * CELL, 2 * channels)
    copies = pl.pallas_call(
        bands_kernel,
        out_shape=jax.ShapeDtypeStruct((frames_on // 2,) + packed, BF16),
        scratch_shapes=[pltpu.VMEM((LANES + 2 * CELL, 2 * channels), F32)],
        **hint(8),
    )(own, earlier, own_too, earlier_too)
    along = [list(range(core, frames_on, 2)) for core in range(2)]
    cores = [[i, i + 1] for i in range(0, frames_on, 2)]
    frames = lax.all_to_all(copies, "tm", 0, 0, tiled=True, axis_index_groups=along)
    frames = lax.all_gather(frames, "tm", axis_index_groups=cores)

    outs = conv_upsample.shape[2]
    rows_here = BANDS * BAND
    partial = pl.pallas_call(
        upsample_kernel,
        out_shape=jax.ShapeDtypeStruct((rows_here, LANES, outs), BF16),
        scratch_shapes=[pltpu.VMEM((9, BANDS, (BAND + 2) * LANES, 2 * channels), BF16)],
        compiler_params=pltpu.CompilerParams(vmem_limit_bytes=32 * MIB),
    )(frames, moves(), conv_upsample, other)
    groups = [[c for c in range(channels_on) if (c // PAIR) % 2 == half] for half in range(2)]
    parts = lax.all_to_all(partial, "chan", 0, 0, tiled=True, axis_index_groups=groups)
    return pl.pallas_call(
        finish_kernel,
        out_shape=jax.ShapeDtypeStruct((2, outs // 8, 4 * LANES), BF16),
        scratch_shapes=[pltpu.VMEM((outs, LANES), F32)],
        compiler_params=pltpu.CompilerParams(vmem_limit_bytes=16 * MIB),
    )(parts)


def solution(mesh):
    placed = (
        P("tm", "chan", None, None),
        P("chan", None, None),
        P("chan", None, None),
        P(None, "chan", "tm"),
    )
    return jax.shard_map(
        on_device, mesh=mesh, in_specs=placed, out_specs=P("chan", "tm", None), check_vma=False
    )
```

```python
import jax
import jax.numpy as jnp
import numpy as np
from jax import lax
from jax.experimental import pallas as pl
from jax.experimental.pallas import tpu as pltpu
from jax.sharding import PartitionSpec as P

EPSILON = 1e-06
F32 = jnp.float32
BF16 = jnp.bfloat16
COLS = 4
FRAMES = 2
CELL = FRAMES * COLS
LANES = 128
ROWS = 16
PAIR = 4
BAND = 4
BANDS = 2
MIB = 1 << 20


def lane_ids():
    lane = lax.broadcasted_iota(jnp.int32, (1, LANES), 1)
    return lane // CELL, (lane // COLS) % FRAMES, lane % COLS


def spatial_sum(product, first_tap, outs):
    row, _, col = lane_ids()
    total = None
    for row_off in range(3):
        part = None
        for col_off in range(3):
            start = (first_tap + 3 * row_off + col_off) * outs
            piece = product[start : start + outs]
            if col_off == 0:
                piece = jnp.where(col >= 1, pltpu.roll(piece, 1, 1), 0.0)
            if col_off == 2:
                piece = jnp.where(col < COLS - 1, pltpu.roll(piece, LANES - 1, 1), 0.0)
            part = piece if part is None else part + piece
        if row_off == 0:
            part = jnp.where(row >= 1, pltpu.roll(part, CELL, 1), 0.0)
        if row_off == 2:
            part = jnp.where(row < ROWS - 1, pltpu.roll(part, LANES - CELL, 1), 0.0)
        total = part if total is None else total + part
    return total


def start_kernel(latent_ref, places_ref, copies_ref):
    cells = [latent_ref[t, r] for r in range(ROWS) for t in range(FRAMES)]
    places = jnp.concatenate(cells, axis=0).astype(F32).T.astype(BF16)
    places_ref[...] = places
    for i in range(copies_ref.shape[0]):
        copies_ref[i] = places


def block_kernel(whole_ref, weight_ref, *rest):
    *residual, own_ref, later_ref = rest
    depth = whole_ref.shape[0]
    outs = own_ref.shape[0]
    values = whole_ref[...].astype(F32)
    squares = jnp.sum(values * values, axis=0, keepdims=True)
    scaled = values * lax.rsqrt(squares / depth + EPSILON)
    act = (scaled / (1.0 + jnp.exp(-scaled))).astype(BF16)
    product = jnp.dot(weight_ref[...], act, preferred_element_type=F32)
    frame = lane_ids()[1]
    oldest = spatial_sum(product, 0, outs)
    middle = spatial_sum(product, 9, outs)
    newest = spatial_sum(product, 18, outs)
    first = lax.axis_index("tm") == 0
    start = jnp.where(frame == 0, middle + oldest, pltpu.roll(oldest, COLS, 1))
    own = newest + jnp.where(frame == 1, pltpu.roll(middle, COLS, 1), 0.0)
    own = own + jnp.where(first, start, 0.0)
    for ref in residual:
        own = ref[...].astype(F32) + own
    own_ref[...] = own
    later_ref[...] = oldest + jnp.where(frame == 0, pltpu.roll(middle, LANES - COLS, 1), 0.0)


def block_conv(whole, weight, outs, *residual):
    shape = jax.ShapeDtypeStruct((outs, LANES), F32)
    return pl.pallas_call(
        block_kernel,
        out_shape=(shape, shape),
        compiler_params=pltpu.CompilerParams(vmem_limit_bytes=16 * MIB),
        cost_estimate=pl.CostEstimate(flops=4 * 10**9, bytes_accessed=8 * MIB, transcendentals=0),
    )(whole, weight, *residual)


def next_frames(i):
    return (i + 1) % lax.axis_size("tm")


def shifted_on(later):
    return lax.ppermute(later, "tm", [(i, next_frames(i)) for i in range(lax.axis_size("tm"))])


def swapped(value):
    return lax.ppermute(value, "chan", [(c, c ^ PAIR) for c in range(lax.axis_size("chan"))])


def shifted_and_swapped(later):
    frames, channels = lax.axis_size("tm"), lax.axis_size("chan")
    pairs = [
        (i * channels + c, next_frames(i) * channels + (c ^ PAIR))
        for i in range(frames)
        for c in range(channels)
    ]
    return lax.ppermute(later, ("tm", "chan"), pairs)


def summed(own_ref, earlier_ref):
    earlier = jnp.where(lax.axis_index("tm") == 0, 0.0, earlier_ref[...])
    return (own_ref[...] + earlier).astype(BF16)


def hidden_kernel(own_ref, earlier_ref, copies_ref):
    value = summed(own_ref, earlier_ref)
    for i in range(copies_ref.shape[0]):
        copies_ref[i] = value


def middle():
    place = lax.axis_index("chan") // PAIR
    return (place == 1) | (place == 2)


def bands_kernel(own_ref, earlier_ref, own_too_ref, earlier_too_ref, copies_ref):
    both = [summed(own_ref, earlier_ref), summed(own_too_ref, earlier_too_ref)]
    places = jnp.concatenate([v.astype(F32).T for v in both], axis=1)
    near, far = (BAND - 1) * CELL, (3 * BAND - 1) * CELL
    count = copies_ref.shape[1]
    inner = places[near : near + count]
    outer = jnp.concatenate([places[far:], places[: count - (LANES - far)]], axis=0)
    value = jnp.where(middle(), inner, outer).astype(BF16)
    for i in range(copies_ref.shape[0]):
        copies_ref[i] = value


def hint(limit):
    return {
        "compiler_params": pltpu.CompilerParams(vmem_limit_bytes=limit * MIB),
        "cost_estimate": pl.CostEstimate(flops=8 * 10**9, bytes_accessed=MIB, transcendentals=0),
    }


def upsample_kernel(all_ref, move_ref, weight_ref, weight_too_ref, out_ref, moved):
    count = 2 * all_ref.shape[1]
    channels = all_ref.shape[3]
    inner = jnp.where(middle(), 1.0, 0.0).astype(BF16)
    for row in range(0, BANDS * BAND + 2, 2):
        places = []
        for r in (row, row + 1):
            cells = [
                all_ref[i % 2, i // 2, r * CELL : (r + 1) * CELL].astype(F32)
                for i in range(count)
            ]
            places.append(jnp.concatenate(cells, axis=0))
        pair = jnp.concatenate(places, axis=1).astype(BF16)
        result = jnp.dot(move_ref[...], pair, preferred_element_type=F32).astype(BF16)
        for k in range(9):
            for j in range(2):
                piece = result[k * LANES : (k + 1) * LANES, j * channels : (j + 1) * channels]
                for band in range(BANDS):
                    at = row + j - band * BAND
                    if 0 <= at < BAND + 2:
                        seam = at == (BAND + 1 if band == 0 else 0)
                        moved[k, band, at * LANES : (at + 1) * LANES] = (
                            piece * inner if seam else piece
                        )
    blocks = []
    for tap in range(27):
        blocks.append(weight_ref[tap])
        blocks.append(weight_too_ref[tap])
    weight = jnp.concatenate(blocks, axis=0)
    for band in range(BANDS):
        spread = jnp.concatenate(
            [
                moved[3 * kt + ks, band, kr * LANES : (kr + BAND) * LANES]
                for kt in range(3)
                for kr in range(3)
                for ks in range(3)
            ],
            axis=1,
        )
        result = jnp.dot(spread, weight, preferred_element_type=F32).astype(BF16)
        for r in range(BAND):
            out_ref[band * BAND + r] = result[r * LANES : (r + 1) * LANES]


def moves():
    place = np.arange(LANES)
    frame, col = place // COLS, place % COLS
    blocks = []
    for frame_off in range(3):
        for col_off in range(3):
            target = col + col_off - 1
            source = np.maximum(frame + frame_off - 2, 0) * COLS + target
            fits = (target >= 0) & (target < COLS)
            blocks.append(fits[:, None] & (source[:, None] == place[None, :]))
    return np.concatenate(blocks, axis=0).astype(jnp.bfloat16)


def finish_kernel(parts_ref, spread_ref, out_ref, total_ref):
    count = parts_ref.shape[0]
    channels = out_ref.shape[1]
    total = parts_ref[0].astype(F32)
    for i in range(1, count):
        total = total + parts_ref[i].astype(F32)
    total_ref[...] = total.T
    halves = []
    for p2 in range(2):
        pieces = [
            total_ref[pl.ds(4 * p1 + 2 * p2 + p3, channels, stride=8), :]
            for p1 in range(2)
            for p3 in range(2)
        ]
        halves.append(jnp.concatenate(pieces, axis=1))
    value = jnp.concatenate(halves, axis=0).astype(BF16)
    result = jnp.dot(value, spread_ref[...], preferred_element_type=F32).astype(BF16)
    for p2 in range(2):
        out_ref[p2] = result[p2 * channels : (p2 + 1) * channels]


def spreads():
    place = np.arange(LANES)
    target = np.arange(4 * LANES)
    base = (place // COLS) * (4 * COLS) + (place % COLS) * 2
    blocks = []
    for p1 in range(2):
        for p3 in range(2):
            blocks.append((base + 2 * COLS * p1 + p3)[:, None] == target[None, :])
    return np.concatenate(blocks, axis=0).astype(jnp.bfloat16)


def on_device(latent, conv_first, conv_second, conv_upsample):
    channels = latent.shape[1]
    frames_on, channels_on = lax.axis_size("tm"), lax.axis_size("chan")

    def taps(weight):
        outs, count, depth = weight.shape
        return jnp.transpose(weight, (1, 0, 2)).reshape(count * outs, depth)

    shape = (channels, LANES)
    places, copies = pl.pallas_call(
        start_kernel,
        out_shape=(
            jax.ShapeDtypeStruct(shape, BF16),
            jax.ShapeDtypeStruct((channels_on,) + shape, BF16),
        ),
        **hint(8),
    )(jnp.transpose(latent, (0, 2, 3, 1)))
    whole = lax.all_to_all(copies, "chan", 0, 0, tiled=True).reshape(-1, LANES)

    own, later = block_conv(whole, taps(conv_first), channels)
    copies = pl.pallas_call(
        hidden_kernel, out_shape=jax.ShapeDtypeStruct((channels_on,) + shape, BF16), **hint(8)
    )(own, shifted_on(later))
    whole = lax.all_to_all(copies, "chan", 0, 0, tiled=True).reshape(-1, LANES)

    own, later = block_conv(whole, taps(conv_second), channels, places)
    own_too = swapped(own)
    earlier_too = shifted_and_swapped(later)
    earlier = shifted_on(later)
    earlier_too, other = lax.optimization_barrier((earlier_too, conv_upsample))
    other = swapped(other)
    packed = ((BANDS * BAND + 2) * CELL, 2 * channels)
    copies = pl.pallas_call(
        bands_kernel,
        out_shape=jax.ShapeDtypeStruct((frames_on // 2,) + packed, BF16),
        **hint(8),
    )(own, earlier, own_too, earlier_too)
    along = [list(range(core, frames_on, 2)) for core in range(2)]
    cores = [[i, i + 1] for i in range(0, frames_on, 2)]
    frames = lax.all_to_all(copies, "tm", 0, 0, tiled=True, axis_index_groups=along)
    frames = lax.all_gather(frames, "tm", axis_index_groups=cores)

    outs = conv_upsample.shape[2]
    rows_here = BANDS * BAND
    partial = pl.pallas_call(
        upsample_kernel,
        out_shape=jax.ShapeDtypeStruct((rows_here, LANES, outs), BF16),
        scratch_shapes=[pltpu.VMEM((9, BANDS, (BAND + 2) * LANES, 2 * channels), BF16)],
        compiler_params=pltpu.CompilerParams(vmem_limit_bytes=32 * MIB),
    )(frames, moves(), conv_upsample, other)
    groups = [
        [place * PAIR + c for place in pair for c in range(PAIR)] for pair in ((1, 2), (3, 0))
    ]
    parts = lax.all_to_all(partial, "chan", 0, 0, tiled=True, axis_index_groups=groups)
    return pl.pallas_call(
        finish_kernel,
        out_shape=jax.ShapeDtypeStruct((2, outs // 8, 4 * LANES), BF16),
        scratch_shapes=[pltpu.VMEM((outs, LANES), F32)],
        compiler_params=pltpu.CompilerParams(vmem_limit_bytes=16 * MIB),
    )(parts, spreads())


def solution(mesh):
    placed = (
        P("tm", "chan", None, None),
        P("chan", None, None),
        P("chan", None, None),
        P(None, "chan", "tm"),
    )
    return jax.shard_map(
        on_device, mesh=mesh, in_specs=placed, out_specs=P("chan", "tm", None), check_vma=False
    )
```

```python
import jax
import jax.numpy as jnp
import numpy as np
from jax import lax
from jax.experimental import pallas as pl
from jax.experimental.pallas import tpu as pltpu
from jax.sharding import PartitionSpec as P

EPSILON = 1e-06
F32 = jnp.float32
BF16 = jnp.bfloat16
COLS = 4
FRAMES = 2
CELL = FRAMES * COLS
LANES = 128
ROWS = 16
PAIR = 4
BAND = 4
BANDS = 2
MIB = 1 << 20


def lane_ids():
    lane = lax.broadcasted_iota(jnp.int32, (1, LANES), 1)
    return lane // CELL, (lane // COLS) % FRAMES, lane % COLS


def spatial_sum(product, first_tap, outs):
    row, _, col = lane_ids()
    total = None
    for row_off in range(3):
        part = None
        for col_off in range(3):
            start = (first_tap + 3 * row_off + col_off) * outs
            piece = product[start : start + outs]
            if col_off == 0:
                piece = jnp.where(col >= 1, pltpu.roll(piece, 1, 1), 0.0)
            if col_off == 2:
                piece = jnp.where(col < COLS - 1, pltpu.roll(piece, LANES - 1, 1), 0.0)
            part = piece if part is None else part + piece
        if row_off == 0:
            part = jnp.where(row >= 1, pltpu.roll(part, CELL, 1), 0.0)
        if row_off == 2:
            part = jnp.where(row < ROWS - 1, pltpu.roll(part, LANES - CELL, 1), 0.0)
        total = part if total is None else total + part
    return total


def start_kernel(latent_ref, places_ref, copies_ref):
    places = latent_ref[...].astype(F32).T.astype(BF16)
    places_ref[...] = places
    for i in range(copies_ref.shape[0]):
        copies_ref[i] = places


def block_kernel(whole_ref, weight_ref, *rest):
    *residual, own_ref, later_ref = rest
    depth = whole_ref.shape[0]
    outs = own_ref.shape[0]
    values = whole_ref[...].astype(F32)
    squares = jnp.sum(values * values, axis=0, keepdims=True)
    scaled = values * lax.rsqrt(squares / depth + EPSILON)
    act = (scaled / (1.0 + jnp.exp(-scaled))).astype(BF16)
    product = jnp.dot(weight_ref[...], act, preferred_element_type=F32)
    frame = lane_ids()[1]
    oldest = spatial_sum(product, 0, outs)
    middle = spatial_sum(product, 9, outs)
    newest = spatial_sum(product, 18, outs)
    first = lax.axis_index("tm") == 0
    start = jnp.where(frame == 0, middle + oldest, pltpu.roll(oldest, COLS, 1))
    own = newest + jnp.where(frame == 1, pltpu.roll(middle, COLS, 1), 0.0)
    own = own + jnp.where(first, start, 0.0)
    for ref in residual:
        own = ref[...].astype(F32) + own
    own_ref[...] = own
    later_ref[...] = oldest + jnp.where(frame == 0, pltpu.roll(middle, LANES - COLS, 1), 0.0)


def block_conv(whole, weight, outs, *residual):
    shape = jax.ShapeDtypeStruct((outs, LANES), F32)
    return pl.pallas_call(
        block_kernel,
        out_shape=(shape, shape),
        compiler_params=pltpu.CompilerParams(vmem_limit_bytes=16 * MIB),
        cost_estimate=pl.CostEstimate(flops=4 * 10**9, bytes_accessed=8 * MIB, transcendentals=0),
    )(whole, weight, *residual)


def next_frames(i):
    return (i + 1) % lax.axis_size("tm")


def shifted_on(later):
    return lax.ppermute(later, "tm", [(i, next_frames(i)) for i in range(lax.axis_size("tm"))])


def swapped(value):
    return lax.ppermute(value, "chan", [(c, c ^ PAIR) for c in range(lax.axis_size("chan"))])


def shifted_and_swapped(later):
    frames, channels = lax.axis_size("tm"), lax.axis_size("chan")
    pairs = [
        (i * channels + c, next_frames(i) * channels + (c ^ PAIR))
        for i in range(frames)
        for c in range(channels)
    ]
    return lax.ppermute(later, ("tm", "chan"), pairs)


def summed(own_ref, earlier_ref):
    earlier = jnp.where(lax.axis_index("tm") == 0, 0.0, earlier_ref[...])
    return (own_ref[...] + earlier).astype(BF16)


def hidden_kernel(own_ref, earlier_ref, copies_ref):
    value = summed(own_ref, earlier_ref)
    for i in range(copies_ref.shape[0]):
        copies_ref[i] = value


def middle():
    place = lax.axis_index("chan") // PAIR
    return (place == 1) | (place == 2)


def bands_kernel(own_ref, earlier_ref, own_too_ref, earlier_too_ref, copies_ref):
    both = [summed(own_ref, earlier_ref), summed(own_too_ref, earlier_too_ref)]
    places = jnp.concatenate([v.astype(F32).T for v in both], axis=1)
    near, far = (BAND - 1) * CELL, (3 * BAND - 1) * CELL
    count = copies_ref.shape[1]
    inner = places[near : near + count]
    outer = jnp.concatenate([places[far:], places[: count - (LANES - far)]], axis=0)
    value = jnp.where(middle(), inner, outer).astype(BF16)
    for i in range(copies_ref.shape[0]):
        copies_ref[i] = value


def hint(limit):
    return {
        "compiler_params": pltpu.CompilerParams(vmem_limit_bytes=limit * MIB),
        "cost_estimate": pl.CostEstimate(flops=8 * 10**9, bytes_accessed=MIB, transcendentals=0),
    }


def upsample_kernel(all_ref, move_ref, weight_ref, weight_too_ref, out_ref, moved):
    count = 2 * all_ref.shape[1]
    channels = all_ref.shape[3]
    inner = jnp.where(middle(), 1.0, 0.0).astype(BF16)
    for row in range(0, BANDS * BAND + 2, 2):
        cells = [
            all_ref[i % 2, i // 2, row * CELL : (row + 2) * CELL].astype(F32)
            for i in range(count)
        ]
        places = [
            jnp.concatenate([cell[j * CELL : (j + 1) * CELL] for cell in cells], axis=0)
            for j in range(2)
        ]
        pair = jnp.concatenate(places, axis=1).astype(BF16)
        result = jnp.dot(move_ref[...], pair, preferred_element_type=F32)
        blocks = [result[k * LANES : (k + 1) * LANES] for k in range(6)]
        blocks = [
            jnp.concatenate([block[:COLS], block[:COLS], block[: LANES - CELL]], axis=0)
            for block in blocks[3:]
        ] + blocks
        for k in range(9):
            block = blocks[k].astype(BF16)
            for j in range(2):
                piece = block[:, j * channels : (j + 1) * channels]
                for band in range(BANDS):
                    at = row + j - band * BAND
                    if 0 <= at < BAND + 2:
                        seam = at == (BAND + 1 if band == 0 else 0)
                        moved[k, band, at * LANES : (at + 1) * LANES] = (
                            piece * inner if seam else piece
                        )
    blocks = []
    for tap in range(27):
        blocks.append(weight_ref[tap])
        blocks.append(weight_too_ref[tap])
    weight = jnp.concatenate(blocks, axis=0)
    for band in range(BANDS):
        spread = jnp.concatenate(
            [
                moved[3 * kt + ks, band, kr * LANES : (kr + BAND) * LANES]
                for kt in range(3)
                for kr in range(3)
                for ks in range(3)
            ],
            axis=1,
        )
        result = jnp.dot(spread, weight, preferred_element_type=F32).astype(BF16)
        for r in range(BAND):
            out_ref[band * BAND + r] = result[r * LANES : (r + 1) * LANES]


def moves():
    place = np.arange(LANES)
    frame, col = place // COLS, place % COLS
    blocks = []
    for frame_off in (1, 2):
        for col_off in range(3):
            target = col + col_off - 1
            source = np.maximum(frame + frame_off - 2, 0) * COLS + target
            fits = (target >= 0) & (target < COLS)
            blocks.append(fits[:, None] & (source[:, None] == place[None, :]))
    return np.concatenate(blocks, axis=0).astype(jnp.bfloat16)


def finish_kernel(parts_ref, spread_ref, out_ref, total_ref):
    count = parts_ref.shape[0]
    channels = out_ref.shape[1]
    total = parts_ref[0].astype(F32)
    for i in range(1, count):
        total = total + parts_ref[i].astype(F32)
    total_ref[...] = total.T
    halves = []
    for p2 in range(2):
        pieces = [
            total_ref[pl.ds(4 * p1 + 2 * p2 + p3, channels, stride=8), :]
            for p1 in range(2)
            for p3 in range(2)
        ]
        halves.append(jnp.concatenate(pieces, axis=1))
    value = jnp.concatenate(halves, axis=0).astype(BF16)
    result = jnp.dot(value, spread_ref[...], preferred_element_type=F32).astype(BF16)
    for p2 in range(2):
        out_ref[p2] = result[p2 * channels : (p2 + 1) * channels]


def spreads():
    place = np.arange(LANES)
    target = np.arange(4 * LANES)
    base = (place // COLS) * (4 * COLS) + (place % COLS) * 2
    blocks = []
    for p1 in range(2):
        for p3 in range(2):
            blocks.append((base + 2 * COLS * p1 + p3)[:, None] == target[None, :])
    return np.concatenate(blocks, axis=0).astype(jnp.bfloat16)


def on_device(latent, conv_first, conv_second, conv_upsample):
    channels = latent.shape[1]
    frames_on, channels_on = lax.axis_size("tm"), lax.axis_size("chan")

    def taps(weight):
        outs, count, depth = weight.shape
        return jnp.transpose(weight, (1, 0, 2)).reshape(count * outs, depth)

    shape = (channels, LANES)
    places, copies = pl.pallas_call(
        start_kernel,
        out_shape=(
            jax.ShapeDtypeStruct(shape, BF16),
            jax.ShapeDtypeStruct((channels_on,) + shape, BF16),
        ),
        **hint(8),
    )(jnp.transpose(latent, (2, 0, 3, 1)).reshape(LANES, channels))
    whole = lax.all_to_all(copies, "chan", 0, 0, tiled=True).reshape(-1, LANES)

    own, later = block_conv(whole, taps(conv_first), channels)
    copies = pl.pallas_call(
        hidden_kernel, out_shape=jax.ShapeDtypeStruct((channels_on,) + shape, BF16), **hint(8)
    )(own, shifted_on(later))
    whole = lax.all_to_all(copies, "chan", 0, 0, tiled=True).reshape(-1, LANES)

    own, later = block_conv(whole, taps(conv_second), channels, places)
    own_too = swapped(own)
    earlier_too = shifted_and_swapped(later)
    earlier = shifted_on(later)
    earlier_too, other = lax.optimization_barrier((earlier_too, conv_upsample))
    other = swapped(other)
    packed = ((BANDS * BAND + 2) * CELL, 2 * channels)
    copies = pl.pallas_call(
        bands_kernel,
        out_shape=jax.ShapeDtypeStruct((frames_on // 2,) + packed, BF16),
        **hint(8),
    )(own, earlier, own_too, earlier_too)
    along = [list(range(core, frames_on, 2)) for core in range(2)]
    cores = [[i, i + 1] for i in range(0, frames_on, 2)]
    frames = lax.all_to_all(copies, "tm", 0, 0, tiled=True, axis_index_groups=along)
    frames = lax.all_gather(frames, "tm", axis_index_groups=cores)

    outs = conv_upsample.shape[2]
    rows_here = BANDS * BAND
    partial = pl.pallas_call(
        upsample_kernel,
        out_shape=jax.ShapeDtypeStruct((rows_here, LANES, outs), BF16),
        scratch_shapes=[pltpu.VMEM((9, BANDS, (BAND + 2) * LANES, 2 * channels), BF16)],
        compiler_params=pltpu.CompilerParams(vmem_limit_bytes=32 * MIB),
    )(frames, moves(), conv_upsample, other)
    groups = [
        [place * PAIR + c for place in pair for c in range(PAIR)] for pair in ((1, 2), (3, 0))
    ]
    parts = lax.all_to_all(partial, "chan", 0, 0, tiled=True, axis_index_groups=groups)
    return pl.pallas_call(
        finish_kernel,
        out_shape=jax.ShapeDtypeStruct((2, outs // 8, 4 * LANES), BF16),
        scratch_shapes=[pltpu.VMEM((outs, LANES), F32)],
        compiler_params=pltpu.CompilerParams(vmem_limit_bytes=16 * MIB),
    )(parts, spreads())


def solution(mesh):
    placed = (
        P("tm", "chan", None, None),
        P("chan", None, None),
        P("chan", None, None),
        P(None, "chan", "tm"),
    )
    return jax.shard_map(
        on_device, mesh=mesh, in_specs=placed, out_specs=P("chan", "tm", None), check_vma=False
    )
```

```python
import jax
import jax.numpy as jnp
import numpy as np
from jax import lax
from jax.experimental import pallas as pl
from jax.experimental.pallas import tpu as pltpu
from jax.sharding import PartitionSpec as P

EPSILON = 1e-06
F32 = jnp.float32
BF16 = jnp.bfloat16
COLS = 4
FRAMES = 2
CELL = FRAMES * COLS
LANES = 128
ROWS = 16
PAIR = 4
BAND = 4
BANDS = 2
MIB = 1 << 20


def lane_ids():
    lane = lax.broadcasted_iota(jnp.int32, (1, LANES), 1)
    return lane // CELL, (lane // COLS) % FRAMES, lane % COLS


def spatial_sum(product, first_tap, outs):
    row, _, col = lane_ids()
    total = None
    for row_off in range(3):
        part = None
        for col_off in range(3):
            start = (first_tap + 3 * row_off + col_off) * outs
            piece = product[start : start + outs]
            if col_off == 0:
                piece = jnp.where(col >= 1, pltpu.roll(piece, 1, 1), 0.0)
            if col_off == 2:
                piece = jnp.where(col < COLS - 1, pltpu.roll(piece, LANES - 1, 1), 0.0)
            part = piece if part is None else part + piece
        if row_off == 0:
            part = jnp.where(row >= 1, pltpu.roll(part, CELL, 1), 0.0)
        if row_off == 2:
            part = jnp.where(row < ROWS - 1, pltpu.roll(part, LANES - CELL, 1), 0.0)
        total = part if total is None else total + part
    return total


def start_kernel(latent_ref, places_ref, copies_ref):
    places = latent_ref[...].astype(F32).T.astype(BF16)
    places_ref[...] = places
    for i in range(copies_ref.shape[0]):
        copies_ref[i] = places


def block_kernel(whole_ref, weight_ref, *rest):
    *residual, own_ref, later_ref = rest
    depth = whole_ref.shape[0]
    outs = own_ref.shape[0]
    values = whole_ref[...].astype(F32)
    squares = jnp.sum(values * values, axis=0, keepdims=True)
    scaled = values * lax.rsqrt(squares / depth + EPSILON)
    act = (scaled / (1.0 + jnp.exp(-scaled))).astype(BF16)
    product = jnp.dot(weight_ref[...], act, preferred_element_type=F32)
    frame = lane_ids()[1]
    oldest = spatial_sum(product, 0, outs)
    middle = spatial_sum(product, 9, outs)
    newest = spatial_sum(product, 18, outs)
    first = lax.axis_index("tm") == 0
    start = jnp.where(frame == 0, middle + oldest, pltpu.roll(oldest, COLS, 1))
    own = newest + jnp.where(frame == 1, pltpu.roll(middle, COLS, 1), 0.0)
    own = own + jnp.where(first, start, 0.0)
    for ref in residual:
        own = ref[...].astype(F32) + own
    own_ref[...] = own
    later_ref[...] = oldest + jnp.where(frame == 0, pltpu.roll(middle, LANES - COLS, 1), 0.0)


def block_conv(whole, weight, outs, *residual):
    shape = jax.ShapeDtypeStruct((outs, LANES), F32)
    return pl.pallas_call(
        block_kernel,
        out_shape=(shape, shape),
        compiler_params=pltpu.CompilerParams(vmem_limit_bytes=16 * MIB),
        cost_estimate=pl.CostEstimate(flops=4 * 10**9, bytes_accessed=8 * MIB, transcendentals=0),
    )(whole, weight, *residual)


def next_frames(i):
    return (i + 1) % lax.axis_size("tm")


def shifted_on(later):
    return lax.ppermute(later, "tm", [(i, next_frames(i)) for i in range(lax.axis_size("tm"))])


def swapped(value):
    return lax.ppermute(value, "chan", [(c, c ^ PAIR) for c in range(lax.axis_size("chan"))])


def shifted_and_swapped(later):
    frames, channels = lax.axis_size("tm"), lax.axis_size("chan")
    pairs = [
        (i * channels + c, next_frames(i) * channels + (c ^ PAIR))
        for i in range(frames)
        for c in range(channels)
    ]
    return lax.ppermute(later, ("tm", "chan"), pairs)


def summed(own_ref, earlier_ref):
    earlier = jnp.where(lax.axis_index("tm") == 0, 0.0, earlier_ref[...])
    return (own_ref[...] + earlier).astype(BF16)


def hidden_kernel(own_ref, earlier_ref, copies_ref):
    value = summed(own_ref, earlier_ref)
    for i in range(copies_ref.shape[0]):
        copies_ref[i] = value


def middle():
    place = lax.axis_index("chan") // PAIR
    return (place == 1) | (place == 2)


def bands_kernel(own_ref, earlier_ref, own_too_ref, earlier_too_ref, copies_ref):
    both = [summed(own_ref, earlier_ref), summed(own_too_ref, earlier_too_ref)]
    places = jnp.concatenate([v.astype(F32).T for v in both], axis=1)
    near, far = (BAND - 1) * CELL, (3 * BAND - 1) * CELL
    count = copies_ref.shape[1]
    inner = places[near : near + count]
    outer = jnp.concatenate([places[far:], places[: count - (LANES - far)]], axis=0)
    value = jnp.where(middle(), inner, outer).astype(BF16)
    for i in range(copies_ref.shape[0]):
        copies_ref[i] = value


def hint(limit):
    return {
        "compiler_params": pltpu.CompilerParams(vmem_limit_bytes=limit * MIB),
        "cost_estimate": pl.CostEstimate(flops=8 * 10**9, bytes_accessed=MIB, transcendentals=0),
    }


def upsample_kernel(here_ref, there_ref, move_ref, weight_ref, weight_too_ref, out_ref, moved):
    chips, _, channels = here_ref.shape
    low = lax.axis_index("tm") % 2 == 0
    inner = jnp.where(middle(), 1.0, 0.0).astype(BF16)
    for row in range(0, BANDS * BAND + 2, 2):
        cells = []
        for i in range(chips):
            here = here_ref[i, row * CELL : (row + 2) * CELL].astype(F32)
            there = there_ref[i, row * CELL : (row + 2) * CELL].astype(F32)
            cells += [jnp.where(low, here, there), jnp.where(low, there, here)]
        places = [
            jnp.concatenate([cell[j * CELL : (j + 1) * CELL] for cell in cells], axis=0)
            for j in range(2)
        ]
        pair = jnp.concatenate(places, axis=1).astype(BF16)
        result = jnp.dot(move_ref[...], pair, preferred_element_type=F32)
        blocks = [result[k * LANES : (k + 1) * LANES] for k in range(6)]
        blocks = [
            jnp.concatenate([block[:COLS], block[:COLS], block[: LANES - CELL]], axis=0)
            for block in blocks[3:]
        ] + blocks
        for k in range(9):
            block = blocks[k].astype(BF16)
            for j in range(2):
                piece = block[:, j * channels : (j + 1) * channels]
                for band in range(BANDS):
                    at = row + j - band * BAND
                    if 0 <= at < BAND + 2:
                        seam = at == (BAND + 1 if band == 0 else 0)
                        moved[k, band, at * LANES : (at + 1) * LANES] = (
                            piece * inner if seam else piece
                        )
    blocks = []
    for tap in range(27):
        blocks.append(weight_ref[tap])
        blocks.append(weight_too_ref[tap])
    weight = jnp.concatenate(blocks, axis=0)
    for band in range(BANDS):
        spread = jnp.concatenate(
            [
                moved[3 * kt + ks, band, kr * LANES : (kr + BAND) * LANES]
                for kt in range(3)
                for kr in range(3)
                for ks in range(3)
            ],
            axis=1,
        )
        result = jnp.dot(spread, weight, preferred_element_type=F32).astype(BF16)
        for r in range(BAND):
            out_ref[band * BAND + r] = result[r * LANES : (r + 1) * LANES]


def moves():
    place = np.arange(LANES)
    frame, col = place // COLS, place % COLS
    blocks = []
    for frame_off in (1, 2):
        for col_off in range(3):
            target = col + col_off - 1
            source = np.maximum(frame + frame_off - 2, 0) * COLS + target
            fits = (target >= 0) & (target < COLS)
            blocks.append(fits[:, None] & (source[:, None] == place[None, :]))
    return np.concatenate(blocks, axis=0).astype(jnp.bfloat16)


def finish_kernel(parts_ref, spread_ref, out_ref, total_ref):
    count = parts_ref.shape[0]
    channels = out_ref.shape[1]
    total = parts_ref[0].astype(F32)
    for i in range(1, count):
        total = total + parts_ref[i].astype(F32)
    total_ref[...] = total.T
    halves = []
    for p2 in range(2):
        pieces = [
            total_ref[pl.ds(4 * p1 + 2 * p2 + p3, channels, stride=8), :]
            for p1 in range(2)
            for p3 in range(2)
        ]
        halves.append(jnp.concatenate(pieces, axis=1))
    value = jnp.concatenate(halves, axis=0).astype(BF16)
    result = jnp.dot(value, spread_ref[...], preferred_element_type=F32).astype(BF16)
    for p2 in range(2):
        out_ref[p2] = result[p2 * channels : (p2 + 1) * channels]


def spreads():
    place = np.arange(LANES)
    target = np.arange(4 * LANES)
    base = (place // COLS) * (4 * COLS) + (place % COLS) * 2
    blocks = []
    for p1 in range(2):
        for p3 in range(2):
            blocks.append((base + 2 * COLS * p1 + p3)[:, None] == target[None, :])
    return np.concatenate(blocks, axis=0).astype(jnp.bfloat16)


def on_device(latent, conv_first, conv_second, conv_upsample):
    channels = latent.shape[1]
    frames_on, channels_on = lax.axis_size("tm"), lax.axis_size("chan")

    def taps(weight):
        outs, count, depth = weight.shape
        return jnp.transpose(weight, (1, 0, 2)).reshape(count * outs, depth)

    shape = (channels, LANES)
    places, copies = pl.pallas_call(
        start_kernel,
        out_shape=(
            jax.ShapeDtypeStruct(shape, BF16),
            jax.ShapeDtypeStruct((channels_on,) + shape, BF16),
        ),
        **hint(8),
    )(jnp.transpose(latent, (2, 0, 3, 1)).reshape(LANES, channels))
    whole = lax.all_to_all(copies, "chan", 0, 0, tiled=True).reshape(-1, LANES)

    own, later = block_conv(whole, taps(conv_first), channels)
    copies = pl.pallas_call(
        hidden_kernel, out_shape=jax.ShapeDtypeStruct((channels_on,) + shape, BF16), **hint(8)
    )(own, shifted_on(later))
    whole = lax.all_to_all(copies, "chan", 0, 0, tiled=True).reshape(-1, LANES)

    own, later = block_conv(whole, taps(conv_second), channels, places)
    own_too = swapped(own)
    earlier_too = shifted_and_swapped(later)
    earlier = shifted_on(later)
    earlier_too, other = lax.optimization_barrier((earlier_too, conv_upsample))
    other = swapped(other)
    packed = ((BANDS * BAND + 2) * CELL, 2 * channels)
    copies = pl.pallas_call(
        bands_kernel,
        out_shape=jax.ShapeDtypeStruct((frames_on // 2,) + packed, BF16),
        **hint(8),
    )(own, earlier, own_too, earlier_too)
    along = [list(range(core, frames_on, 2)) for core in range(2)]
    frames = lax.all_to_all(copies, "tm", 0, 0, tiled=True, axis_index_groups=along)
    frames_too = lax.ppermute(frames, "tm", [(i, i ^ 1) for i in range(frames_on)])

    outs = conv_upsample.shape[2]
    rows_here = BANDS * BAND
    partial = pl.pallas_call(
        upsample_kernel,
        out_shape=jax.ShapeDtypeStruct((rows_here, LANES, outs), BF16),
        scratch_shapes=[pltpu.VMEM((9, BANDS, (BAND + 2) * LANES, 2 * channels), BF16)],
        compiler_params=pltpu.CompilerParams(vmem_limit_bytes=32 * MIB),
    )(frames, frames_too, moves(), conv_upsample, other)
    groups = [
        [place * PAIR + c for place in pair for c in range(PAIR)] for pair in ((1, 2), (3, 0))
    ]
    parts = lax.all_to_all(partial, "chan", 0, 0, tiled=True, axis_index_groups=groups)
    return pl.pallas_call(
        finish_kernel,
        out_shape=jax.ShapeDtypeStruct((2, outs // 8, 4 * LANES), BF16),
        scratch_shapes=[pltpu.VMEM((outs, LANES), F32)],
        compiler_params=pltpu.CompilerParams(vmem_limit_bytes=16 * MIB),
    )(parts, spreads())


def solution(mesh):
    placed = (
        P("tm", "chan", None, None),
        P("chan", None, None),
        P("chan", None, None),
        P(None, "chan", "tm"),
    )
    return jax.shard_map(
        on_device, mesh=mesh, in_specs=placed, out_specs=P("chan", "tm", None), check_vma=False
    )
```

```python
import jax
import jax.numpy as jnp
import numpy as np
from jax import lax
from jax.experimental import pallas as pl
from jax.experimental.pallas import tpu as pltpu
from jax.sharding import PartitionSpec as P

EPSILON = 1e-06
F32 = jnp.float32
BF16 = jnp.bfloat16
COLS = 4
FRAMES = 2
CELL = FRAMES * COLS
LANES = 128
ROWS = 16
PAIR = 4
BAND = 4
BANDS = 2
MIB = 1 << 20


def lane_ids():
    lane = lax.broadcasted_iota(jnp.int32, (1, LANES), 1)
    return lane // CELL, (lane // COLS) % FRAMES, lane % COLS


def spatial_sum(product, first_tap, outs):
    row, _, col = lane_ids()
    total = None
    for row_off in range(3):
        part = None
        for col_off in range(3):
            start = (first_tap + 3 * row_off + col_off) * outs
            piece = product[start : start + outs]
            if col_off == 0:
                piece = jnp.where(col >= 1, pltpu.roll(piece, 1, 1), 0.0)
            if col_off == 2:
                piece = jnp.where(col < COLS - 1, pltpu.roll(piece, LANES - 1, 1), 0.0)
            part = piece if part is None else part + piece
        if row_off == 0:
            part = jnp.where(row >= 1, pltpu.roll(part, CELL, 1), 0.0)
        if row_off == 2:
            part = jnp.where(row < ROWS - 1, pltpu.roll(part, LANES - CELL, 1), 0.0)
        total = part if total is None else total + part
    return total


def start_kernel(latent_ref, places_ref, copies_ref):
    places = latent_ref[...].astype(F32).T.astype(BF16)
    places_ref[...] = places
    for i in range(copies_ref.shape[0]):
        copies_ref[i] = places


def later_kernel(whole_ref, weight_ref, act_ref, middle_ref, later_ref):
    depth = whole_ref.shape[0]
    outs = later_ref.shape[0]
    values = whole_ref[...].astype(F32)
    squares = jnp.sum(values * values, axis=0, keepdims=True)
    half = values * (0.5 * lax.rsqrt(squares / depth + EPSILON))
    act = (half + half * jnp.tanh(half)).astype(BF16)
    act_ref[...] = act
    product = jnp.dot(weight_ref[: 18 * outs], act, preferred_element_type=F32)
    frame = lane_ids()[1]
    oldest = spatial_sum(product, 0, outs)
    middle = spatial_sum(product, 9, outs)
    first = lax.axis_index("tm") == 0
    start = jnp.where(frame == 0, middle + oldest, pltpu.roll(oldest, COLS, 1))
    own = jnp.where(frame == 1, pltpu.roll(middle, COLS, 1), 0.0)
    middle_ref[...] = own + jnp.where(first, start, 0.0)
    later_ref[...] = oldest + jnp.where(frame == 0, pltpu.roll(middle, LANES - COLS, 1), 0.0)


def own_kernel(act_ref, weight_ref, *rest):
    *parts, own_ref = rest
    outs = own_ref.shape[0]
    product = jnp.dot(weight_ref[18 * outs :], act_ref[...], preferred_element_type=F32)
    own = spatial_sum(product, 0, outs)
    for ref in parts:
        own = ref[...].astype(F32) + own
    own_ref[...] = own


def work(limit, flops):
    return {
        "compiler_params": pltpu.CompilerParams(vmem_limit_bytes=limit * MIB),
        "cost_estimate": pl.CostEstimate(flops=flops, bytes_accessed=MIB, transcendentals=0),
    }


def block_conv(whole, weight, outs, *residual):
    shape = jax.ShapeDtypeStruct((outs, LANES), F32)
    act, middle, later = pl.pallas_call(
        later_kernel,
        out_shape=(jax.ShapeDtypeStruct(whole.shape, BF16), shape, shape),
        **work(16, 4 * 10**9),
    )(whole, weight)
    own = pl.pallas_call(own_kernel, out_shape=shape, **work(16, 2 * 10**9))(
        act, weight, middle, *residual
    )
    return own, later


def next_frames(i):
    return (i + 1) % lax.axis_size("tm")


def shifted_on(later):
    return lax.ppermute(later, "tm", [(i, next_frames(i)) for i in range(lax.axis_size("tm"))])


def swapped(value):
    return lax.ppermute(value, "chan", [(c, c ^ PAIR) for c in range(lax.axis_size("chan"))])


def shifted_and_swapped(later):
    frames, channels = lax.axis_size("tm"), lax.axis_size("chan")
    pairs = [
        (i * channels + c, next_frames(i) * channels + (c ^ PAIR))
        for i in range(frames)
        for c in range(channels)
    ]
    return lax.ppermute(later, ("tm", "chan"), pairs)


def summed(own_ref, earlier_ref):
    earlier = jnp.where(lax.axis_index("tm") == 0, 0.0, earlier_ref[...])
    return (own_ref[...] + earlier).astype(BF16)


def hidden_kernel(own_ref, earlier_ref, copies_ref):
    value = summed(own_ref, earlier_ref)
    for i in range(copies_ref.shape[0]):
        copies_ref[i] = value


def middle():
    place = lax.axis_index("chan") // PAIR
    return (place == 1) | (place == 2)


def bands_kernel(own_ref, earlier_ref, own_too_ref, earlier_too_ref, copies_ref):
    both = [summed(own_ref, earlier_ref), summed(own_too_ref, earlier_too_ref)]
    places = jnp.concatenate([v.astype(F32).T for v in both], axis=1)
    near, far = (BAND - 1) * CELL, (3 * BAND - 1) * CELL
    count = copies_ref.shape[1]
    inner = places[near : near + count]
    outer = jnp.concatenate([places[far:], places[: count - (LANES - far)]], axis=0)
    value = jnp.where(middle(), inner, outer).astype(BF16)
    for i in range(copies_ref.shape[0]):
        copies_ref[i] = value


def hint(limit):
    return {
        "compiler_params": pltpu.CompilerParams(vmem_limit_bytes=limit * MIB),
        "cost_estimate": pl.CostEstimate(flops=8 * 10**9, bytes_accessed=MIB, transcendentals=0),
    }


def moved_kernel(here_ref, there_ref, move_ref, moved):
    chips, _, channels = here_ref.shape
    low = lax.axis_index("tm") % 2 == 0
    inner = jnp.where(middle(), 1.0, 0.0).astype(BF16)
    for row in range(0, BANDS * BAND + 2, 2):
        cells = []
        for i in range(chips):
            here = here_ref[i, row * CELL : (row + 2) * CELL].astype(F32)
            there = there_ref[i, row * CELL : (row + 2) * CELL].astype(F32)
            cells += [jnp.where(low, here, there), jnp.where(low, there, here)]
        places = [
            jnp.concatenate([cell[j * CELL : (j + 1) * CELL] for cell in cells], axis=0)
            for j in range(2)
        ]
        pair = jnp.concatenate(places, axis=1).astype(BF16)
        result = jnp.dot(move_ref[...], pair, preferred_element_type=F32)
        blocks = [result[k * LANES : (k + 1) * LANES] for k in range(6)]
        blocks = [
            jnp.concatenate([block[:COLS], block[:COLS], block[: LANES - CELL]], axis=0)
            for block in blocks[3:]
        ] + blocks
        for k in range(9):
            block = blocks[k].astype(BF16)
            for j in range(2):
                piece = block[:, j * channels : (j + 1) * channels]
                for band in range(BANDS):
                    at = row + j - band * BAND
                    if 0 <= at < BAND + 2:
                        seam = at == (BAND + 1 if band == 0 else 0)
                        moved[k, band, at * LANES : (at + 1) * LANES] = (
                            piece * inner if seam else piece
                        )


def upsample_kernel(moved, weight_ref, weight_too_ref, out_ref):
    blocks = []
    for tap in range(27):
        blocks.append(weight_ref[tap])
        blocks.append(weight_too_ref[tap])
    weight = jnp.concatenate(blocks, axis=0)
    for band in range(BANDS):
        spread = jnp.concatenate(
            [
                moved[3 * kt + ks, band, kr * LANES : (kr + BAND) * LANES]
                for kt in range(3)
                for kr in range(3)
                for ks in range(3)
            ],
            axis=1,
        )
        result = jnp.dot(spread, weight, preferred_element_type=F32).astype(BF16)
        for r in range(BAND):
            out_ref[band * BAND + r] = result[r * LANES : (r + 1) * LANES]


def moves():
    place = np.arange(LANES)
    frame, col = place // COLS, place % COLS
    blocks = []
    for frame_off in (1, 2):
        for col_off in range(3):
            target = col + col_off - 1
            source = np.maximum(frame + frame_off - 2, 0) * COLS + target
            fits = (target >= 0) & (target < COLS)
            blocks.append(fits[:, None] & (source[:, None] == place[None, :]))
    return np.concatenate(blocks, axis=0).astype(jnp.bfloat16)


def finish_kernel(parts_ref, spread_ref, out_ref, total_ref):
    count = parts_ref.shape[0]
    channels = out_ref.shape[1]
    total = parts_ref[0].astype(F32)
    for i in range(1, count):
        total = total + parts_ref[i].astype(F32)
    total_ref[...] = total.T
    halves = []
    for p2 in range(2):
        pieces = [
            total_ref[pl.ds(4 * p1 + 2 * p2 + p3, channels, stride=8), :]
            for p1 in range(2)
            for p3 in range(2)
        ]
        halves.append(jnp.concatenate(pieces, axis=1))
    value = jnp.concatenate(halves, axis=0).astype(BF16)
    result = jnp.dot(value, spread_ref[...], preferred_element_type=F32).astype(BF16)
    for p2 in range(2):
        out_ref[p2] = result[p2 * channels : (p2 + 1) * channels]


def spreads():
    place = np.arange(LANES)
    target = np.arange(4 * LANES)
    base = (place // COLS) * (4 * COLS) + (place % COLS) * 2
    blocks = []
    for p1 in range(2):
        for p3 in range(2):
            blocks.append((base + 2 * COLS * p1 + p3)[:, None] == target[None, :])
    return np.concatenate(blocks, axis=0).astype(jnp.bfloat16)


def on_device(latent, conv_first, conv_second, conv_upsample):
    channels = latent.shape[1]
    frames_on, channels_on = lax.axis_size("tm"), lax.axis_size("chan")

    def taps(weight):
        outs, count, depth = weight.shape
        return jnp.transpose(weight, (1, 0, 2)).reshape(count * outs, depth)

    shape = (channels, LANES)
    places, copies = pl.pallas_call(
        start_kernel,
        out_shape=(
            jax.ShapeDtypeStruct(shape, BF16),
            jax.ShapeDtypeStruct((channels_on,) + shape, BF16),
        ),
        **hint(8),
    )(jnp.transpose(latent, (2, 0, 3, 1)).reshape(LANES, channels))
    whole = lax.all_to_all(copies, "chan", 0, 0, tiled=True).reshape(-1, LANES)

    own, later = block_conv(whole, taps(conv_first), channels)
    copies = pl.pallas_call(
        hidden_kernel, out_shape=jax.ShapeDtypeStruct((channels_on,) + shape, BF16), **hint(8)
    )(own, shifted_on(later))
    whole = lax.all_to_all(copies, "chan", 0, 0, tiled=True).reshape(-1, LANES)

    own, later = block_conv(whole, taps(conv_second), channels, places)
    own_too = swapped(own)
    earlier_too = shifted_and_swapped(later)
    earlier = shifted_on(later)
    earlier_too, other = lax.optimization_barrier((earlier_too, conv_upsample))
    other = swapped(other)
    packed = ((BANDS * BAND + 2) * CELL, 2 * channels)
    copies = pl.pallas_call(
        bands_kernel,
        out_shape=jax.ShapeDtypeStruct((frames_on // 2,) + packed, BF16),
        **hint(8),
    )(own, earlier, own_too, earlier_too)
    along = [list(range(core, frames_on, 2)) for core in range(2)]
    frames = lax.all_to_all(copies, "tm", 0, 0, tiled=True, axis_index_groups=along)
    frames_too = lax.ppermute(frames, "tm", [(i, i ^ 1) for i in range(frames_on)])

    outs = conv_upsample.shape[2]
    rows_here = BANDS * BAND
    moved = pl.pallas_call(
        moved_kernel,
        out_shape=jax.ShapeDtypeStruct((9, BANDS, (BAND + 2) * LANES, 2 * channels), BF16),
        compiler_params=pltpu.CompilerParams(vmem_limit_bytes=16 * MIB),
    )(frames, frames_too, moves())
    partial = pl.pallas_call(
        upsample_kernel,
        out_shape=jax.ShapeDtypeStruct((rows_here, LANES, outs), BF16),
        compiler_params=pltpu.CompilerParams(vmem_limit_bytes=24 * MIB),
    )(moved, conv_upsample, other)
    groups = [
        [place * PAIR + c for place in pair for c in range(PAIR)] for pair in ((1, 2), (3, 0))
    ]
    parts = lax.all_to_all(partial, "chan", 0, 0, tiled=True, axis_index_groups=groups)
    return pl.pallas_call(
        finish_kernel,
        out_shape=jax.ShapeDtypeStruct((2, outs // 8, 4 * LANES), BF16),
        scratch_shapes=[pltpu.VMEM((outs, LANES), F32)],
        compiler_params=pltpu.CompilerParams(vmem_limit_bytes=16 * MIB),
    )(parts, spreads())


def solution(mesh):
    placed = (
        P("tm", "chan", None, None),
        P("chan", None, None),
        P("chan", None, None),
        P(None, "chan", "tm"),
    )
    return jax.shard_map(
        on_device, mesh=mesh, in_specs=placed, out_specs=P("chan", "tm", None), check_vma=False
    )
```

```python
import jax
import jax.numpy as jnp
import numpy as np
from jax import lax
from jax.experimental import pallas as pl
from jax.experimental.pallas import tpu as pltpu
from jax.sharding import PartitionSpec as P

EPSILON = 1e-06
F32 = jnp.float32
BF16 = jnp.bfloat16
COLS = 4
FRAMES = 2
CELL = FRAMES * COLS
LANES = 128
ROWS = 16
PAIR = 4
BAND = 4
BANDS = 2
MIB = 1 << 20


def lane_ids():
    lane = lax.broadcasted_iota(jnp.int32, (1, LANES), 1)
    return lane // CELL, (lane // COLS) % FRAMES, lane % COLS


def spatial_sum(product, first_tap, outs):
    row, _, col = lane_ids()
    total = None
    for row_off in range(3):
        part = None
        for col_off in range(3):
            start = (first_tap + 3 * row_off + col_off) * outs
            piece = product[start : start + outs]
            if col_off == 0:
                piece = jnp.where(col >= 1, pltpu.roll(piece, 1, 1), 0.0)
            if col_off == 2:
                piece = jnp.where(col < COLS - 1, pltpu.roll(piece, LANES - 1, 1), 0.0)
            part = piece if part is None else part + piece
        if row_off == 0:
            part = jnp.where(row >= 1, pltpu.roll(part, CELL, 1), 0.0)
        if row_off == 2:
            part = jnp.where(row < ROWS - 1, pltpu.roll(part, LANES - CELL, 1), 0.0)
        total = part if total is None else total + part
    return total


def start_kernel(latent_ref, places_ref, copies_ref):
    places = latent_ref[...].astype(F32).T.astype(BF16)
    places_ref[...] = places
    for i in range(copies_ref.shape[0]):
        copies_ref[i] = places


def later_kernel(whole_ref, weight_ref, act_ref, middle_ref, later_ref):
    depth = whole_ref.shape[0]
    outs = later_ref.shape[0]
    values = whole_ref[...].astype(F32)
    squares = jnp.sum(values * values, axis=0, keepdims=True)
    scaled = values * lax.rsqrt(squares / depth + EPSILON)
    act = (scaled / (1.0 + jnp.exp(-scaled))).astype(BF16)
    act_ref[...] = act
    product = jnp.dot(weight_ref[: 18 * outs], act, preferred_element_type=F32)
    frame = lane_ids()[1]
    oldest = spatial_sum(product, 0, outs)
    middle = spatial_sum(product, 9, outs)
    first = lax.axis_index("tm") == 0
    start = jnp.where(frame == 0, middle + oldest, pltpu.roll(oldest, COLS, 1))
    own = jnp.where(frame == 1, pltpu.roll(middle, COLS, 1), 0.0)
    middle_ref[...] = own + jnp.where(first, start, 0.0)
    later_ref[...] = oldest + jnp.where(frame == 0, pltpu.roll(middle, LANES - COLS, 1), 0.0)


def own_kernel(act_ref, weight_ref, *rest):
    *parts, own_ref = rest
    outs = own_ref.shape[0]
    product = jnp.dot(weight_ref[18 * outs :], act_ref[...], preferred_element_type=F32)
    own = spatial_sum(product, 0, outs)
    for ref in parts:
        own = ref[...].astype(F32) + own
    own_ref[...] = own


def work(limit, flops):
    return {
        "compiler_params": pltpu.CompilerParams(vmem_limit_bytes=limit * MIB),
        "cost_estimate": pl.CostEstimate(flops=flops, bytes_accessed=MIB, transcendentals=0),
    }


def block_conv(whole, weight, outs, *residual):
    shape = jax.ShapeDtypeStruct((outs, LANES), F32)
    act, middle, later = pl.pallas_call(
        later_kernel,
        out_shape=(jax.ShapeDtypeStruct(whole.shape, BF16), shape, shape),
        **work(16, 4 * 10**9),
    )(whole, weight)
    own = pl.pallas_call(own_kernel, out_shape=shape, **work(16, 2 * 10**9))(
        act, weight, middle, *residual
    )
    return own, later


def next_frames(i):
    return (i + 1) % lax.axis_size("tm")


def shifted_on(later):
    return lax.ppermute(later, "tm", [(i, next_frames(i)) for i in range(lax.axis_size("tm"))])


def swapped(value):
    return lax.ppermute(value, "chan", [(c, c ^ PAIR) for c in range(lax.axis_size("chan"))])


def shifted_and_swapped(later):
    frames, channels = lax.axis_size("tm"), lax.axis_size("chan")
    pairs = [
        (i * channels + c, next_frames(i) * channels + (c ^ PAIR))
        for i in range(frames)
        for c in range(channels)
    ]
    return lax.ppermute(later, ("tm", "chan"), pairs)


def summed(own_ref, earlier_ref):
    earlier = jnp.where(lax.axis_index("tm") == 0, 0.0, earlier_ref[...])
    return (own_ref[...] + earlier).astype(BF16)


def hidden_kernel(own_ref, earlier_ref, copies_ref):
    value = summed(own_ref, earlier_ref)
    for i in range(copies_ref.shape[0]):
        copies_ref[i] = value


def middle():
    place = lax.axis_index("chan") // PAIR
    return (place == 1) | (place == 2)


def bands_kernel(own_ref, earlier_ref, own_too_ref, earlier_too_ref, copies_ref):
    both = [summed(own_ref, earlier_ref), summed(own_too_ref, earlier_too_ref)]
    places = jnp.concatenate([v.astype(F32).T for v in both], axis=1)
    near, far = (BAND - 1) * CELL, (3 * BAND - 1) * CELL
    count = copies_ref.shape[1]
    inner = places[near : near + count]
    outer = jnp.concatenate([places[far:], places[: count - (LANES - far)]], axis=0)
    value = jnp.where(middle(), inner, outer).astype(BF16)
    for i in range(copies_ref.shape[0]):
        copies_ref[i] = value


def hint(limit):
    return {
        "compiler_params": pltpu.CompilerParams(vmem_limit_bytes=limit * MIB),
        "cost_estimate": pl.CostEstimate(flops=8 * 10**9, bytes_accessed=MIB, transcendentals=0),
    }


def moved_kernel(here_ref, there_ref, move_ref, moved):
    chips, _, channels = here_ref.shape
    low = lax.axis_index("tm") % 2 == 0
    inner = jnp.where(middle(), 1.0, 0.0).astype(BF16)
    for row in range(0, BANDS * BAND + 2, 2):
        cells = []
        for i in range(chips):
            here = here_ref[i, row * CELL : (row + 2) * CELL].astype(F32)
            there = there_ref[i, row * CELL : (row + 2) * CELL].astype(F32)
            cells += [jnp.where(low, here, there), jnp.where(low, there, here)]
        places = [
            jnp.concatenate([cell[j * CELL : (j + 1) * CELL] for cell in cells], axis=0)
            for j in range(2)
        ]
        pair = jnp.concatenate(places, axis=1).astype(BF16)
        result = jnp.dot(move_ref[...], pair, preferred_element_type=F32)
        blocks = [result[k * LANES : (k + 1) * LANES] for k in range(6)]
        blocks = [
            jnp.concatenate([block[:COLS], block[:COLS], block[: LANES - CELL]], axis=0)
            for block in blocks[3:]
        ] + blocks
        for k in range(9):
            block = blocks[k].astype(BF16)
            for j in range(2):
                piece = block[:, j * channels : (j + 1) * channels]
                for band in range(BANDS):
                    at = row + j - band * BAND
                    if 0 <= at < BAND + 2:
                        seam = at == (BAND + 1 if band == 0 else 0)
                        moved[k, band, at * LANES : (at + 1) * LANES] = (
                            piece * inner if seam else piece
                        )


def upsample_kernel(moved, weight_ref, weight_too_ref, out_ref):
    blocks = []
    for tap in range(27):
        blocks.append(weight_ref[tap])
        blocks.append(weight_too_ref[tap])
    weight = jnp.concatenate(blocks, axis=0)
    for band in range(BANDS):
        spread = jnp.concatenate(
            [
                moved[3 * kt + ks, band, kr * LANES : (kr + BAND) * LANES]
                for kt in range(3)
                for kr in range(3)
                for ks in range(3)
            ],
            axis=1,
        )
        result = jnp.dot(spread, weight, preferred_element_type=F32).astype(BF16)
        for r in range(BAND):
            out_ref[band * BAND + r] = result[r * LANES : (r + 1) * LANES]


def moves():
    place = np.arange(LANES)
    frame, col = place // COLS, place % COLS
    blocks = []
    for frame_off in (1, 2):
        for col_off in range(3):
            target = col + col_off - 1
            source = np.maximum(frame + frame_off - 2, 0) * COLS + target
            fits = (target >= 0) & (target < COLS)
            blocks.append(fits[:, None] & (source[:, None] == place[None, :]))
    return np.concatenate(blocks, axis=0).astype(jnp.bfloat16)


def finish_kernel(parts_ref, spread_ref, out_ref, total_ref):
    count = parts_ref.shape[0]
    channels = out_ref.shape[1]
    total = parts_ref[0].astype(F32)
    for i in range(1, count):
        total = total + parts_ref[i].astype(F32)
    total_ref[...] = total.T
    halves = []
    for p2 in range(2):
        pieces = [
            total_ref[pl.ds(4 * p1 + 2 * p2 + p3, channels, stride=8), :]
            for p1 in range(2)
            for p3 in range(2)
        ]
        halves.append(jnp.concatenate(pieces, axis=1))
    value = jnp.concatenate(halves, axis=0).astype(BF16)
    result = jnp.dot(value, spread_ref[...], preferred_element_type=F32).astype(BF16)
    for p2 in range(2):
        out_ref[p2] = result[p2 * channels : (p2 + 1) * channels]


def spreads():
    place = np.arange(LANES)
    target = np.arange(4 * LANES)
    base = (place // COLS) * (4 * COLS) + (place % COLS) * 2
    blocks = []
    for p1 in range(2):
        for p3 in range(2):
            blocks.append((base + 2 * COLS * p1 + p3)[:, None] == target[None, :])
    return np.concatenate(blocks, axis=0).astype(jnp.bfloat16)


def on_device(latent, conv_first, conv_second, conv_upsample):
    channels = latent.shape[1]
    frames_on, channels_on = lax.axis_size("tm"), lax.axis_size("chan")

    def taps(weight):
        outs, count, depth = weight.shape
        return jnp.transpose(weight, (1, 0, 2)).reshape(count * outs, depth)

    shape = (channels, LANES)
    places, copies = pl.pallas_call(
        start_kernel,
        out_shape=(
            jax.ShapeDtypeStruct(shape, BF16),
            jax.ShapeDtypeStruct((channels_on,) + shape, BF16),
        ),
        **hint(8),
    )(jnp.transpose(latent, (2, 0, 3, 1)).reshape(LANES, channels))
    whole = lax.all_to_all(copies, "chan", 0, 0, tiled=True).reshape(-1, LANES)

    own, later = block_conv(whole, taps(conv_first), channels)
    copies = pl.pallas_call(
        hidden_kernel, out_shape=jax.ShapeDtypeStruct((channels_on,) + shape, BF16), **hint(8)
    )(own, shifted_on(later))
    whole = lax.all_to_all(copies, "chan", 0, 0, tiled=True).reshape(-1, LANES)

    own, later = block_conv(whole, taps(conv_second), channels, places)
    own_too = swapped(own)
    earlier_too = shifted_and_swapped(later)
    earlier = shifted_on(later)
    earlier_too, other = lax.optimization_barrier((earlier_too, conv_upsample))
    other = swapped(other)
    packed = ((BANDS * BAND + 2) * CELL, 2 * channels)
    copies = pl.pallas_call(
        bands_kernel,
        out_shape=jax.ShapeDtypeStruct((frames_on // 2,) + packed, BF16),
        **hint(8),
    )(own, earlier, own_too, earlier_too)
    along = [list(range(core, frames_on, 2)) for core in range(2)]
    frames = lax.all_to_all(copies, "tm", 0, 0, tiled=True, axis_index_groups=along)
    frames_too = lax.ppermute(frames, "tm", [(i, i ^ 1) for i in range(frames_on)])

    outs = conv_upsample.shape[2]
    rows_here = BANDS * BAND
    moved = pl.pallas_call(
        moved_kernel,
        out_shape=jax.ShapeDtypeStruct((9, BANDS, (BAND + 2) * LANES, 2 * channels), BF16),
        compiler_params=pltpu.CompilerParams(vmem_limit_bytes=16 * MIB),
    )(frames, frames_too, moves())
    partial = pl.pallas_call(
        upsample_kernel,
        out_shape=jax.ShapeDtypeStruct((rows_here, LANES, outs), BF16),
        compiler_params=pltpu.CompilerParams(vmem_limit_bytes=24 * MIB),
    )(moved, conv_upsample, other)
    groups = [
        [place * PAIR + c for place in pair for c in range(PAIR)] for pair in ((1, 2), (3, 0))
    ]
    parts = lax.all_to_all(partial, "chan", 0, 0, tiled=True, axis_index_groups=groups)
    return pl.pallas_call(
        finish_kernel,
        out_shape=jax.ShapeDtypeStruct((2, outs // 8, 4 * LANES), BF16),
        scratch_shapes=[pltpu.VMEM((outs, LANES), F32)],
        compiler_params=pltpu.CompilerParams(vmem_limit_bytes=16 * MIB),
    )(parts, spreads())


def solution(mesh):
    placed = (
        P("tm", "chan", None, None),
        P("chan", None, None),
        P("chan", None, None),
        P(None, "chan", "tm"),
    )
    return jax.shard_map(
        on_device, mesh=mesh, in_specs=placed, out_specs=P("chan", "tm", None), check_vma=False
    )
```
